32 devices in a mesh: expert: 8 (over z, x), tensor: 4 (over y, core).
Axes of the slice: x: 2, y: 2, z: 4, core: 2. Of those that a mesh axis runs over, the one named last changes fastest.
Arguments:
- query_latent: bfloat16 [256, 64, 576], P(('expert', 'tensor')), may hold values from -9 to 9
- kv_cache: bfloat16 [256, 768, 576], P(('expert', 'tensor')), may hold values from -4 to 4
- cache_len: int32 [256], P(('expert', 'tensor')), may hold values from 192 to 768, as said below
- value_up: bfloat16 [64, 512, 128], P('tensor'), may hold values from -0.25 to 0.25
- hidden_in: bfloat16 [256, 7168], P('expert', 'tensor'), may hold values from -6 to 6
- norm_gain: bfloat16 [7168], P('tensor'), may hold values from 0.099609375 to 1.8984375
- expert_ids: int32 [256, 8], P('expert'), may hold values from 0 to 7, all different within a row; in each aligned block of 32 rows (0 to 31, 32 to 63, ...) at most 32 rows name the same one
- route_weight: int32 [256, 8], P('expert'), may hold values from 1 to 4095
- placement_plan: int32 [8], replicated, may hold values from 0 to 7, as said below
- updated_list: int32 [8], replicated, may hold values from 0 to 7, each once
- learner_gate: bfloat16 [8, 7168, 1024], P(None, 'expert', 'tensor'), may hold values from -0.0625 to 0.0625
- learner_up: bfloat16 [8, 7168, 1024], P(None, 'expert', 'tensor'), may hold values from -0.0625 to 0.0625
- learner_down: bfloat16 [8, 7168, 1024], P(None, 'expert', 'tensor'), may hold values from -0.1875 to 0.1875
Outputs:
- attn_values: bfloat16 [256, 8192], P('expert', 'tensor')
- moe_out: bfloat16 [256, 7168], P('expert', 'tensor')
- slot_gate: bfloat16 [8, 7168, 1024], P('expert', None, 'tensor')
The draws below stay inside these ranges and needn't reach their ends.
Inputs may be any that keep to these rules, and one draw needn't show every extreme that they name: `cache_len`: some row has all 768 positions valid. `placement_plan`: every expert is held by one or two slots; 0 experts by two. `expert_ids`: each row names 8 different experts; among the 32 rows of one device no expert is named more than 32 times. `updated_list`: each expert once.
All inputs are finite; a program needn't handle non-finite values.
Results may differ from the reference program's by a relative error of at most 0.015.
Values may be sent and summed in bfloat16 or wider, within the bound.
A program may use at most 128 MiB of HBM per device.

```python
import math
import jax
import jax.numpy as jnp
import numpy as np
from jax import lax

D = 7168
FFN = 1024
HEADS = 64
KVL = 512
VH = 128
TOP = 8
ROWS_DEV = 32
CTX = 768
LAT = 576
REDUNDANT = 0
EXPERTS = 8
ROWS = 256
MOST = 32
N_EXPERT = 8
N_TENSOR = 4


def joint_attention(key):
    key_query = jax.random.fold_in(key, 11)
    key_cache = jax.random.fold_in(key, 12)
    query = jnp.clip(jax.random.normal(key_query, (ROWS, HEADS, LAT), jnp.float32), -4.0, 4.0)
    cache = jnp.clip(jax.random.normal(key_cache, (ROWS, CTX, LAT), jnp.float32), -4.0, 4.0)
    return (query, cache)


def draw_query_latent(key, part):
    query, cache = joint_attention(key)
    return query.astype(jnp.bfloat16)


def draw_kv_cache(key, part):
    query, cache = joint_attention(key)
    return cache.astype(jnp.bfloat16)


def draw_cache_len(key, part):
    drawn = jax.random.randint(jax.random.fold_in(key, 31), (ROWS,), CTX // 4, CTX + 1, dtype=jnp.int32)
    return drawn.at[0].set(CTX)


def draw_placement_plan(key, part):
    first = jax.random.permutation(jax.random.fold_in(key, 21), EXPERTS)
    extra = jax.random.permutation(jax.random.fold_in(key, 22), EXPERTS)[:REDUNDANT]
    joined = jnp.concatenate([first, extra]).astype(jnp.int32)
    return jax.random.permutation(jax.random.fold_in(key, 23), joined).astype(jnp.int32)


def touch_ends(values, stream_key, smallest, top_value):
    place = [jax.random.randint(jax.random.fold_in(stream_key, axis), (), 0, length) for axis, length in enumerate(values.shape)]
    widest = values.shape.index(max(values.shape))
    beside = place[:widest] + [(place[widest] + 1) % values.shape[widest]] + place[widest + 1:]
    return values.at[tuple(place)].set(smallest).at[tuple(beside)].set(top_value)


def block_levels(stream_key, dims, cuts, low, high):
    loudness, own = 1.0, jax.random.fold_in(stream_key, 6)
    for axis_at, parts in cuts:
        heights = jnp.exp(jax.random.uniform(jax.random.fold_in(own, axis_at), (parts,), jnp.float32, low / len(cuts), high / len(cuts)))
        loudness = loudness * jnp.repeat(heights, dims[axis_at] // parts).reshape([-1 if axis == axis_at else 1 for axis in range(len(dims))])
    return loudness


def deal_out(own_key, own, number, rows, number_of, top, bound, slope):
    sequence = jax.random.permutation(own_key, number_of)
    heavy_load, ordinary = portions_of(number_of, rows * top, bound, slope, True), portions_of(number_of, rows * top, bound, slope, False)
    places = jnp.arange(number_of)

    def named(lengths, rotation):
        used = int((lengths > 0).sum())
        fixed = max(1, used // 4)
        passed = fixed + (places - fixed + rotation * (used - fixed)) % max(1, number_of - fixed)
        return jnp.zeros((number_of,), jnp.int32).at[sequence[jnp.where(places < fixed, places, passed)]].set(jnp.asarray(lengths, jnp.int32))

    lengths = jnp.where(number % 4 == 0, named(heavy_load, number // 4), named(ordinary, number - number // 4 - 1))
    mixed = jax.random.permutation(jax.random.fold_in(own, 3), number_of)
    source_of, taker = mixed[0:number_of // 2 * 2:2], mixed[1:number_of // 2 * 2:2]
    slack = jnp.minimum(lengths[source_of] - 1, bound - lengths[taker]) // 2
    slack = jnp.where((source_of == sequence[0]) | (taker == sequence[0]) | (lengths[taker] == 0), 0, jnp.maximum(slack, 0))
    passed = jax.random.randint(jax.random.fold_in(own, 4), (number_of // 2,), 0, 1 << 20) % (slack + 1)
    lengths = lengths.at[source_of].add(-passed).at[taker].add(passed)
    items = jnp.searchsorted(jnp.cumsum(lengths), jnp.arange(rows * top), side="right").astype(jnp.int32)
    table = items.reshape(top, rows).T
    table = table[jax.random.permutation(jax.random.fold_in(own, 1), rows)]
    rotation = jax.random.randint(jax.random.fold_in(own, 2), (rows, 1), 0, top)
    return jnp.take_along_axis(table, (jnp.arange(top)[None, :] + rotation) % top, axis=1)


def portions_of(number_of, total, limit, slope, full):
    portions = [(1 << 20) // math.isqrt(standing ** slope) + 1 for standing in range(1, number_of + 1)]
    largest = limit if full else min(limit, max(-(-total // number_of), total * portions[0] // sum(portions)))
    least = 1 if total - largest >= number_of - 1 else 0
    holding, spare = [largest] + [least] * (number_of - 1), total - largest - least * (number_of - 1)
    while spare > 0:
        movable = [i for i in range(1, number_of) if holding[i] < largest] or [i for i in range(1, number_of) if holding[i] < limit]
        whole, budget = sum([portions[i] for i in movable]), spare
        for i in movable:
            more = min(limit - holding[i], max(1, budget * portions[i] // whole), spare)
            holding[i] = holding[i] + more
            spare = spare - more
    return np.array(holding)


def gaussian(stream_key, extent, width, reach, pieces=(), kind=jnp.bfloat16):
    result = width * jax.random.normal(stream_key, extent, jnp.float32)
    if pieces:
        result = result * block_levels(stream_key, extent, pieces, -0.22, 0.18)
    return jnp.clip(result, -reach, reach).astype(kind)


def setup_inputs(seed: int = 0) -> dict:
    seeds = jax.random.split(jax.random.key(seed), 14)
    query_latent = draw_query_latent(jax.random.fold_in(seeds[13], 71), 0)
    kv_cache = draw_kv_cache(jax.random.fold_in(seeds[13], 71), 0)
    cache_len = draw_cache_len(jax.random.fold_in(seeds[13], 71), 0)
    value_up = gaussian(seeds[3], (HEADS, KVL, VH), KVL ** -0.5, 0.25, ((0, 4),))
    hidden_in = gaussian(seeds[4], (ROWS, D), 1.0, 6.0, ((0, 8), (1, 4)))
    norm_gain = jnp.clip(1.0 + 0.18 * jax.random.normal(seeds[5], (D,), jnp.float32), 0.099609375, 1.8984375).astype(jnp.bfloat16)
    expert_ids_keys = jax.random.split(jax.random.fold_in(seeds[6], 1), ROWS // ROWS_DEV)
    expert_ids_turns = jax.random.permutation(jax.random.fold_in(seeds[6], 3), ROWS // ROWS_DEV)
    expert_ids = jax.vmap(lambda own, number: deal_out(jax.random.fold_in(seeds[6], 2), own, number, ROWS_DEV, EXPERTS, TOP, MOST, 2))(expert_ids_keys, expert_ids_turns).reshape((ROWS, TOP))
    route_weight = touch_ends(jax.random.randint(seeds[7], (ROWS, TOP), 1, 4096), jax.random.fold_in(seeds[7], 1), 1, 4095).astype(jnp.int32)
    placement_plan = draw_placement_plan(jax.random.fold_in(seeds[13], 71), 0)
    updated_list = jax.random.permutation(seeds[9], EXPERTS).astype(jnp.int32)
    learner_gate = gaussian(seeds[10], (EXPERTS, D, FFN), D ** -0.5, 0.0625, ((1, 8), (2, 4)))
    learner_up = gaussian(seeds[11], (EXPERTS, D, FFN), D ** -0.5, 0.0625, ((1, 8), (2, 4)))
    learner_down = gaussian(seeds[12], (EXPERTS, D, FFN), FFN ** -0.5, 0.1875, ((1, 8), (2, 4)))
    return dict(query_latent=query_latent, kv_cache=kv_cache, cache_len=cache_len, value_up=value_up, hidden_in=hidden_in, norm_gain=norm_gain, expert_ids=expert_ids, route_weight=route_weight, placement_plan=placement_plan, updated_list=updated_list, learner_gate=learner_gate, learner_up=learner_up, learner_down=learner_down)


SCORE_SCALE = 192.0 ** (-0.5)
ROUTE_SCALE = 2.5
NORM_EPSILON = 1e-06

def attend(query_latent, kv_cache, cache_len):
    scores = jnp.einsum('rhc,rpc->rhp', query_latent.astype(jnp.float32), kv_cache.astype(jnp.float32)) * SCORE_SCALE
    allowed = (jnp.arange(kv_cache.shape[1], dtype=jnp.int32)[None, :] < cache_len[:, None])[:, None, :]
    scores = jnp.where(allowed, scores, -1e+30)
    highest = lax.optimization_barrier(jnp.max(scores, axis=2, keepdims=True))
    lifted = jnp.where(allowed, jnp.exp(scores - highest), 0.0)
    totals = lax.optimization_barrier(jnp.sum(lifted, axis=2, keepdims=True))
    probs = lifted.astype(jnp.bfloat16).astype(jnp.float32)
    mixed = jnp.einsum('rhp,rpc->rhc', probs, kv_cache[:, :, :KVL].astype(jnp.float32))
    return (mixed / totals).astype(jnp.bfloat16)

def reference(query_latent, kv_cache, cache_len, value_up, hidden_in, norm_gain, expert_ids, route_weight, placement_plan, updated_list, learner_gate, learner_up, learner_down):
    block_rows = ROWS_DEV
    block_count = ROWS // block_rows

    def attend_block(block):
        query_block, cache_block, length_block = block
        latent = attend(query_block, cache_block, length_block)
        values = jnp.einsum('rhc,hcv->rhv', latent.astype(jnp.float32), value_up.astype(jnp.float32))
        return values.astype(jnp.bfloat16).reshape(block_rows, HEADS * VH)
    attn_values = lax.map(attend_block, (query_latent.reshape(block_count, block_rows, HEADS, LAT), kv_cache.reshape(block_count, block_rows, CTX, LAT), cache_len.reshape(block_count, block_rows))).reshape(ROWS, HEADS * VH)
    widened = hidden_in.astype(jnp.float32)
    normed = (widened * lax.rsqrt(lax.optimization_barrier(jnp.mean(widened * widened, axis=1, keepdims=True)) + NORM_EPSILON) * norm_gain.astype(jnp.float32)[None, :]).astype(jnp.bfloat16)
    expert_range = jnp.arange(EXPERTS, dtype=jnp.int32)
    source = lax.optimization_barrier(jnp.sum(expert_range[None, :] * (updated_list[None, :] == expert_range[:, None]).astype(jnp.int32), axis=1)).astype(jnp.int32)
    slot_gate = learner_gate[source[placement_plan]]
    entry_total = ROWS * TOP
    flat_ids = expert_ids.reshape(entry_total)
    buffer_rows = N_EXPERT * MOST
    block_width = FFN // N_TENSOR

    def one_expert(carry, expert):
        members = jnp.nonzero(flat_ids == expert, size=buffer_rows, fill_value=entry_total)[0].astype(jnp.int32)
        alive = members < entry_total
        chosen = normed[jnp.where(alive, members, 0) // TOP]
        entry = source[expert]
        gate_proj = jnp.dot(chosen, learner_gate[entry], preferred_element_type=jnp.float32)
        up_proj = jnp.dot(chosen, learner_up[entry], preferred_element_type=jnp.float32)
        activated = (jax.nn.silu(gate_proj) * up_proj).astype(jnp.bfloat16)
        blocks = jnp.einsum('rbh,dbh->rbd', activated.reshape(buffer_rows, N_TENSOR, block_width).astype(jnp.float32), learner_down[entry].reshape(D, N_TENSOR, block_width).astype(jnp.float32))
        rounded = blocks.astype(jnp.bfloat16).astype(jnp.float32)
        expert_out = lax.optimization_barrier(jnp.sum(rounded, axis=1)).astype(jnp.bfloat16)
        return (carry.at[members].set(expert_out, mode='drop'), None)
    entry_out, ignored = lax.scan(one_expert, jnp.zeros((entry_total, D), jnp.bfloat16), expert_range)
    weights_float = route_weight.astype(jnp.float32)
    gates = ROUTE_SCALE * weights_float / lax.optimization_barrier(jnp.sum(weights_float, axis=1, keepdims=True))
    moe_out = lax.optimization_barrier(jnp.sum(gates[:, :, None] * entry_out.reshape(ROWS, TOP, D).astype(jnp.float32), axis=1)).astype(jnp.bfloat16)
    return (attn_values, moe_out, slot_gate)
```

```python
import jax
import jax.numpy as jnp
from jax import lax
from jax.sharding import PartitionSpec as P

KVL = 512


SCORE_SCALE = 192.0 ** (-0.5)
ROUTE_SCALE = 2.5
NORM_EPSILON = 1e-06


def attend(query_latent, kv_cache, cache_len):
    scores = (
        jnp.einsum("rhc,rpc->rhp", query_latent, kv_cache, preferred_element_type=jnp.float32)
        * SCORE_SCALE
    )
    allowed = (jnp.arange(kv_cache.shape[1], dtype=jnp.int32)[None, :] < cache_len[:, None])[
        :, None, :
    ]
    scores = jnp.where(allowed, scores, -1e30)
    highest = jnp.max(scores, axis=2, keepdims=True)
    lifted = jnp.where(allowed, jnp.exp(scores - highest), 0.0)
    totals = jnp.sum(lifted, axis=2, keepdims=True)
    mixed = jnp.einsum(
        "rhp,rpc->rhc",
        lifted.astype(jnp.bfloat16),
        kv_cache[:, :, :KVL],
        preferred_element_type=jnp.float32,
    )
    return (mixed / totals).astype(jnp.bfloat16)


def hand_over(learner, placement_plan, updated_list):
    expert_total, depth, width = learner.shape
    devices = lax.axis_size("expert")
    me = lax.axis_index("expert")
    held_each = placement_plan.shape[0] // devices
    entry_range = jnp.arange(expert_total, dtype=jnp.int32)
    slot_range = jnp.arange(placement_plan.shape[0], dtype=jnp.int32)

    def rows_for(device):
        blocks = []
        for held in range(held_each):
            expert = jnp.sum(jnp.where(slot_range == device * held_each + held, placement_plan, 0))
            entry = jnp.sum(jnp.where(updated_list == expert, entry_range, 0))
            blocks.append(lax.dynamic_slice_in_dim(learner, entry, 1, axis=0))
        return blocks[0] if held_each == 1 else jnp.concatenate(blocks, axis=0)

    held = jnp.zeros((held_each, depth * devices, width), learner.dtype)
    held = lax.dynamic_update_slice_in_dim(held, rows_for(me), me * depth, axis=1)
    arrivals = []
    for step in range(1, devices):
        pairs = [(i, (i + step) % devices) for i in range(devices)]
        block = lax.ppermute(rows_for((me + step) % devices), "expert", pairs)
        arrivals.append(((me - step + devices) % devices, block))
    for origin, block in arrivals:
        held = lax.dynamic_update_slice_in_dim(held, block, origin * depth, axis=1)
    return held


def per_device(
    query_latent,
    kv_cache,
    cache_len,
    value_up,
    hidden_in,
    norm_gain,
    expert_ids,
    route_weight,
    placement_plan,
    updated_list,
    learner_gate,
    learner_up,
    learner_down,
):
    held_gate = hand_over(learner_gate, placement_plan, updated_list)
    widened = hidden_in.astype(jnp.float32)
    squares = lax.psum(jnp.sum(widened * widened, axis=1, keepdims=True), "tensor")
    row_scale = lax.rsqrt(squares / (hidden_in.shape[1] * lax.axis_size("tensor")) + NORM_EPSILON)
    gained = (widened * norm_gain.astype(jnp.float32)[None, :]).astype(jnp.bfloat16)
    whole_rows = lax.all_gather(gained, "tensor", axis=1, tiled=True)
    slices = lax.all_to_all(whole_rows, "expert", split_axis=1, concat_axis=0, tiled=True)
    gate_part = jnp.einsum("rd,edh->reh", slices, learner_gate, preferred_element_type=jnp.float32)
    up_part = jnp.einsum("rd,edh->reh", slices, learner_up, preferred_element_type=jnp.float32)
    gate_sum = lax.psum_scatter(
        gate_part.astype(jnp.bfloat16), "expert", scatter_dimension=0, tiled=True
    )
    up_sum = lax.psum_scatter(
        up_part.astype(jnp.bfloat16), "expert", scatter_dimension=0, tiled=True
    )
    weights_float = route_weight.astype(jnp.float32)
    gates = ROUTE_SCALE * weights_float / jnp.sum(weights_float, axis=1, keepdims=True)
    chosen = (expert_ids[:, :, None] == updated_list[None, None, :]).astype(jnp.float32)
    share = jnp.sum(gates[:, :, None] * chosen, axis=1)
    gate_proj = gate_sum.astype(jnp.float32) * row_scale[:, :, None]
    up_proj = up_sum.astype(jnp.float32) * row_scale[:, :, None]
    activated = (jax.nn.silu(gate_proj) * up_proj * share[:, :, None]).astype(jnp.bfloat16)
    all_activated = lax.all_gather(activated, "expert", axis=0, tiled=True)
    partial_out = jnp.einsum(
        "reh,edh->rd", all_activated, learner_down, preferred_element_type=jnp.float32
    )
    returned = lax.all_to_all(
        partial_out.astype(jnp.bfloat16), "expert", split_axis=0, concat_axis=1, tiled=True
    )
    moe_out = lax.psum_scatter(returned, "tensor", scatter_dimension=1, tiled=True)
    latent = attend(query_latent, kv_cache, cache_len)
    head_rows = lax.all_to_all(latent, "tensor", split_axis=1, concat_axis=0, tiled=True)
    projected = jnp.einsum("rhc,hcv->rhv", head_rows, value_up, preferred_element_type=jnp.float32)
    attn_values = projected.astype(jnp.bfloat16).reshape(
        head_rows.shape[0], projected.shape[1] * projected.shape[2]
    )
    return (attn_values, moe_out, held_gate)


def solution(mesh):
    in_specs = (
        P(("expert", "tensor"), None, None),
        P(("expert", "tensor"), None, None),
        P(("expert", "tensor")),
        P("tensor", None, None),
        P("expert", "tensor"),
        P("tensor"),
        P("expert", None),
        P("expert", None),
        P(),
        P(),
        P(None, "expert", "tensor"),
        P(None, "expert", "tensor"),
        P(None, "expert", "tensor"),
    )
    out_specs = (P("expert", "tensor"), P("expert", "tensor"), P("expert", None, "tensor"))
    return jax.shard_map(
        per_device, mesh=mesh, in_specs=in_specs, out_specs=out_specs, check_vma=False
    )
```

```python
import functools

import jax
import jax.numpy as jnp
from jax import lax
from jax.experimental import pallas as pl
from jax.experimental.pallas import tpu as pltpu
from jax.sharding import PartitionSpec as P

KVL = 512


SCORE_SCALE = 192.0 ** (-0.5)
ROUTE_SCALE = 2.5
NORM_EPSILON = 1e-06


def attend(query_latent, kv_cache, cache_len):
    scores = (
        jnp.einsum("rhc,rpc->rhp", query_latent, kv_cache, preferred_element_type=jnp.float32)
        * SCORE_SCALE
    )
    allowed = (jnp.arange(kv_cache.shape[1], dtype=jnp.int32)[None, :] < cache_len[:, None])[
        :, None, :
    ]
    scores = jnp.where(allowed, scores, -1e30)
    highest = jnp.max(scores, axis=2, keepdims=True)
    lifted = jnp.where(allowed, jnp.exp(scores - highest), 0.0)
    totals = jnp.sum(lifted, axis=2, keepdims=True)
    mixed = jnp.einsum(
        "rhp,rpc->rhc",
        lifted.astype(jnp.bfloat16),
        kv_cache[:, :, :KVL],
        preferred_element_type=jnp.float32,
    )
    return (mixed / totals).astype(jnp.bfloat16)


def pick_entries(learner, entries):
    depth, width = learner.shape[1:]

    def copy(entries_ref, in_ref, out_ref):
        out_ref[...] = in_ref[...]

    return pl.pallas_call(
        copy,
        grid_spec=pltpu.PrefetchScalarGridSpec(
            num_scalar_prefetch=1,
            grid=(entries.shape[0],),
            in_specs=[pl.BlockSpec((1, depth, width), lambda s, e: (e[s], 0, 0))],
            out_specs=pl.BlockSpec((1, depth, width), lambda s, e: (s, 0, 0)),
        ),
        out_shape=jax.ShapeDtypeStruct((entries.shape[0], depth, width), learner.dtype),
    )(entries, learner)


def moe_kernel(
    devices,
    lanes,
    x_ref,
    square_ref,
    share_ref,
    chosen_ref,
    gate_hbm,
    up_hbm,
    down_hbm,
    out_ref,
    held_ref,
    rows,
    squares,
    gate_w,
    up_w,
    down_w,
    parts,
    came,
    acts,
    total,
    leaving,
    back,
    local_sem,
    row_send,
    row_recv,
    square_send,
    square_recv,
    part_send,
    part_recv,
    act_send,
    act_recv,
    back_send,
    back_recv,
    held_send,
    held_recv,
):
    i, t = lax.axis_index("expert"), lax.axis_index("tensor")
    per = devices // lanes
    entries, depth, width = gate_w.shape
    row_count = x_ref.shape[1]
    whole = devices * lanes
    me = i * lanes + t

    def remote(src, dst, send, recv, expert, tensor):
        return pltpu.make_async_remote_copy(
            src_ref=src,
            dst_ref=dst,
            send_sem=send,
            recv_sem=recv,
            device_id=(expert, tensor),
            device_id_type=pl.DeviceIdType.MESH,
        )

    def each(first, last, body):
        lax.fori_loop(first, last, lambda k, c: (body(k), c)[1], 0)

    loads = [
        pltpu.make_async_copy(gate_hbm, gate_w, local_sem.at[0]),
        pltpu.make_async_copy(up_hbm, up_w, local_sem.at[1]),
        pltpu.make_async_copy(down_hbm, down_w, local_sem.at[2]),
    ]
    for load in loads:
        load.start()
    own = pltpu.make_async_copy(chosen_ref.at[i], held_ref.at[i], local_sem.at[3])
    own.start()

    barrier = pltpu.get_barrier_semaphore()

    def greet(k):
        other = lax.rem(me + k, whole)
        pl.semaphore_signal(
            barrier,
            inc=1,
            device_id=(other // lanes, lax.rem(other, lanes)),
            device_id_type=pl.DeviceIdType.MESH,
        )

    each(1, whole, greet)
    pl.semaphore_wait(barrier, whole - 1)

    def row_copy(p, k):
        to = lax.rem(t + k, lanes)
        return remote(
            x_ref.at[p], rows.at[i], row_send.at[p * lanes + k], row_recv.at[i], t * per + p, to
        )

    for p in range(per):
        each(1, lanes, lambda k, p=p: row_copy(p, k).start())
        pl.when(t * per + p != i)(lambda p=p: row_copy(p, 0).start())

    def square_copy(k):
        to = lax.rem(t + k, lanes)
        return remote(square_ref, squares.at[t], square_send.at[k], square_recv.at[t], i, to)

    each(1, lanes, lambda k: square_copy(k).start())

    def held_copy(k):
        to = lax.rem(i + k, devices)
        return remote(
            chosen_ref.at[to], held_ref.at[i], held_send.at[k], held_recv.at[i], to, t
        )

    each(1, devices, lambda k: held_copy(k).start())

    home = i // per

    @pl.when(home == t)
    def _():
        rows[i] = x_ref[lax.rem(i, per)]

    squares[t] = square_ref[...]

    def row_arrival(k):
        origin = lax.rem(i + k, devices)
        remote(
            x_ref.at[0], rows.at[origin], row_send.at[0], row_recv.at[origin], origin, home
        ).wait_recv()

    each(1, devices, row_arrival)
    pl.when(home != t)(lambda: row_arrival(0))
    loads[0].wait()
    loads[1].wait()

    def project(e):
        arrived = rows[...].reshape(devices * row_count, depth)
        for which, weight in enumerate((gate_w, up_w)):
            product = jnp.dot(arrived, weight[e], preferred_element_type=jnp.float32)
            parts[:, which, e] = product.astype(jnp.bfloat16).reshape(devices, row_count, width)

    each(0, entries, project)

    def part_copy(k):
        to = lax.rem(i + k, devices)
        return remote(parts.at[to], came.at[i], part_send.at[k], part_recv.at[i], to, t)

    each(1, devices, lambda k: part_copy(k).start())
    came[i] = parts[i]

    def square_arrival(k):
        origin = lax.rem(t + k, lanes)
        remote(
            square_ref, squares.at[origin], square_send.at[0], square_recv.at[origin], i, origin
        ).wait_recv()

    each(1, lanes, square_arrival)
    features = depth * devices
    row_scale = lax.rsqrt(jnp.sum(squares[...], axis=0) / features + NORM_EPSILON)[:, :1]

    def part_arrival(k):
        origin = lax.rem(i + k, devices)
        remote(
            parts.at[0], came.at[origin], part_send.at[0], part_recv.at[origin], origin, t
        ).wait_recv()

    each(1, devices, part_arrival)

    def activate(e):
        gate = jnp.sum(came[:, 0, e].astype(jnp.float32), axis=0) * row_scale
        up = jnp.sum(came[:, 1, e].astype(jnp.float32), axis=0) * row_scale
        silu = gate / (1.0 + jnp.exp(-gate))
        acts[i, e] = (silu * up * share_ref[e]).astype(jnp.bfloat16)

    each(0, entries, activate)

    def act_copy(k):
        to = lax.rem(i + k, devices)
        return remote(acts.at[i], acts.at[i], act_send.at[k], act_recv.at[i], to, t)

    each(1, devices, lambda k: act_copy(k).start())
    loads[2].wait()

    def act_arrival(k):
        origin = lax.rem(i + k, devices)
        remote(
            acts.at[i], acts.at[origin], act_send.at[0], act_recv.at[origin], origin, t
        ).wait_recv()

    each(1, devices, act_arrival)
    total[...] = jnp.zeros_like(total)

    def lower(e):
        total[...] += lax.dot_general(
            acts[:, e].reshape(devices * row_count, width),
            down_w[e],
            (((1,), (1,)), ((), ())),
            preferred_element_type=jnp.float32,
        )

    each(0, entries, lower)
    leaving[...] = total[...].astype(jnp.bfloat16).reshape(devices, row_count, depth)

    place = lax.rem(i, per) * lanes + t

    def back_copy(k):
        to = lax.rem(i + k, devices)
        return remote(leaving.at[to], back.at[place], back_send.at[k], back_recv.at[place], to, home)

    each(1, devices, lambda k: back_copy(k).start())
    pl.when(home != t)(lambda: back_copy(0).start())

    @pl.when(home == t)
    def _():
        back[place] = leaving[i]

    def back_arrival(p, k):
        lane = lax.rem(t + k, lanes)
        slot = p * lanes + lane
        remote(
            leaving.at[0], back.at[slot], back_send.at[0], back_recv.at[slot], t * per + p, lane
        ).wait_recv()

    for p in range(per):
        each(1, lanes, lambda k, p=p: back_arrival(p, k))
        pl.when(t * per + p != i)(lambda p=p: back_arrival(p, 0))
    for p in range(per):
        summed = jnp.zeros((row_count, depth), jnp.float32)
        for lane in range(lanes):
            summed += back[p * lanes + lane].astype(jnp.float32)
        out_ref[p] = summed.astype(jnp.bfloat16)

    for p in range(per):
        each(1, lanes, lambda k, p=p: row_copy(p, k).wait_send())
        pl.when(t * per + p != i)(lambda p=p: row_copy(p, 0).wait_send())
    each(1, lanes, lambda k: square_copy(k).wait_send())
    each(1, devices, lambda k: part_copy(k).wait_send())
    each(1, devices, lambda k: act_copy(k).wait_send())
    each(1, devices, lambda k: back_copy(k).wait_send())
    pl.when(home != t)(lambda: back_copy(0).wait_send())

    def held_arrival(k):
        origin = lax.rem(i + k, devices)
        remote(
            chosen_ref.at[0], held_ref.at[origin], held_send.at[0], held_recv.at[origin], origin, t
        ).wait_recv()

    each(1, devices, held_arrival)
    each(1, devices, lambda k: held_copy(k).wait_send())
    own.wait()


def moe(x, square, share, chosen, gate, up, down, devices, lanes):
    entries, depth, width = gate.shape
    per, row_count = x.shape[:2]
    held_each = chosen.shape[1]
    vmem = pl.BlockSpec(memory_space=pltpu.VMEM)
    anywhere = pl.BlockSpec(memory_space=pl.ANY)
    bf16 = jnp.bfloat16
    dma = pltpu.SemaphoreType.DMA
    return pl.pallas_call(
        functools.partial(moe_kernel, devices, lanes),
        out_shape=(
            jax.ShapeDtypeStruct((per, row_count, depth), bf16),
            jax.ShapeDtypeStruct((devices, held_each, depth, width), bf16),
        ),
        in_specs=[vmem, vmem, vmem, anywhere, anywhere, anywhere, anywhere],
        out_specs=(vmem, anywhere),
        scratch_shapes=[
            pltpu.VMEM((devices, row_count, depth), bf16),
            pltpu.VMEM((lanes,) + square.shape, jnp.float32),
            pltpu.VMEM(gate.shape, bf16),
            pltpu.VMEM(up.shape, bf16),
            pltpu.VMEM(down.shape, bf16),
            pltpu.VMEM((devices, 2, entries, row_count, width), bf16),
            pltpu.VMEM((devices, 2, entries, row_count, width), bf16),
            pltpu.VMEM((devices, entries, row_count, width), bf16),
            pltpu.VMEM((devices * row_count, depth), jnp.float32),
            pltpu.VMEM((devices, row_count, depth), bf16),
            pltpu.VMEM((per * lanes, row_count, depth), bf16),
            dma((4,)),
            dma((per * lanes,)),
            dma((devices,)),
            dma((lanes,)),
            dma((lanes,)),
            dma((devices,)),
            dma((devices,)),
            dma((devices,)),
            dma((devices,)),
            dma((devices,)),
            dma((per * lanes,)),
            dma((devices,)),
            dma((devices,)),
        ],
        compiler_params=pltpu.CompilerParams(
            collective_id=0, has_side_effects=True, vmem_limit_bytes=60 * 1024 * 1024
        ),
        cost_estimate=pl.CostEstimate(
            flops=6 * devices * row_count * entries * depth * width,
            bytes_accessed=10 * entries * depth * width,
            transcendentals=row_count * entries * width,
        ),
    )(x, square, share, chosen, gate, up, down)


def per_device(
    query_latent,
    kv_cache,
    cache_len,
    value_up,
    hidden_in,
    norm_gain,
    expert_ids,
    route_weight,
    placement_plan,
    updated_list,
    learner_gate,
    learner_up,
    learner_down,
):
    expert_total, depth, width = learner_gate.shape
    devices, lanes = lax.axis_size("expert"), lax.axis_size("tensor")
    per = devices // lanes
    row_count = hidden_in.shape[0]
    slot_total = placement_plan.shape[0]
    held_each = slot_total // devices
    entry_range = jnp.arange(expert_total, dtype=jnp.int32)
    learner_entry = jnp.sum(
        entry_range[None, :] * (updated_list[None, :] == placement_plan[:, None]).astype(jnp.int32),
        axis=1,
    )
    chosen_gate = pick_entries(learner_gate, learner_entry).reshape(
        devices, held_each, depth, width
    )
    widened = hidden_in.astype(jnp.float32)
    square = jnp.broadcast_to(jnp.sum(widened * widened, axis=1, keepdims=True), (row_count, 128))
    gained = (widened * norm_gain.astype(jnp.float32)[None, :]).astype(jnp.bfloat16)
    gained = jnp.swapaxes(gained.reshape(row_count, per, depth), 0, 1)
    weights_float = route_weight.astype(jnp.float32)
    gates = ROUTE_SCALE * weights_float / jnp.sum(weights_float, axis=1, keepdims=True)
    named = (expert_ids[None, :, :] == updated_list[:, None, None]).astype(jnp.float32)
    share = jnp.sum(gates[None, :, :] * named, axis=2)
    share = jnp.broadcast_to(share[:, :, None], (expert_total, row_count, width))
    moe_parts, held = moe(
        gained, square, share, chosen_gate, learner_gate, learner_up, learner_down, devices, lanes
    )
    moe_out = jnp.swapaxes(moe_parts, 0, 1).reshape(row_count, per * depth)
    held_gate = jnp.swapaxes(held, 0, 1).reshape(held_each, devices * depth, width)
    latent = attend(query_latent, kv_cache, cache_len)
    head_rows = lax.all_to_all(latent, "tensor", split_axis=1, concat_axis=0, tiled=True)
    projected = jnp.einsum("rhc,hcv->rhv", head_rows, value_up, preferred_element_type=jnp.float32)
    attn_values = projected.astype(jnp.bfloat16).reshape(
        head_rows.shape[0], projected.shape[1] * projected.shape[2]
    )
    return (attn_values, moe_out, held_gate)


def solution(mesh):
    in_specs = (
        P(("expert", "tensor"), None, None),
        P(("expert", "tensor"), None, None),
        P(("expert", "tensor")),
        P("tensor", None, None),
        P("expert", "tensor"),
        P("tensor"),
        P("expert", None),
        P("expert", None),
        P(),
        P(),
        P(None, "expert", "tensor"),
        P(None, "expert", "tensor"),
        P(None, "expert", "tensor"),
    )
    out_specs = (P("expert", "tensor"), P("expert", "tensor"), P("expert", None, "tensor"))
    return jax.shard_map(
        per_device, mesh=mesh, in_specs=in_specs, out_specs=out_specs, check_vma=False
    )
```

```python
import functools

import jax
import jax.numpy as jnp
from jax import lax
from jax.experimental import pallas as pl
from jax.experimental.pallas import tpu as pltpu
from jax.sharding import PartitionSpec as P

KVL = 512


SCORE_SCALE = 192.0 ** (-0.5)
ROUTE_SCALE = 2.5
NORM_EPSILON = 1e-06


def attend(query_latent, kv_cache, cache_len):
    scores = (
        jnp.einsum("rhc,rpc->rhp", query_latent, kv_cache, preferred_element_type=jnp.float32)
        * SCORE_SCALE
    )
    allowed = (jnp.arange(kv_cache.shape[1], dtype=jnp.int32)[None, :] < cache_len[:, None])[
        :, None, :
    ]
    scores = jnp.where(allowed, scores, -1e30)
    highest = jnp.max(scores, axis=2, keepdims=True)
    lifted = jnp.where(allowed, jnp.exp(scores - highest), 0.0)
    totals = jnp.sum(lifted, axis=2, keepdims=True)
    mixed = jnp.einsum(
        "rhp,rpc->rhc",
        lifted.astype(jnp.bfloat16),
        kv_cache[:, :, :KVL],
        preferred_element_type=jnp.float32,
    )
    return (mixed / totals).astype(jnp.bfloat16)


def pick_entries(learner, entries):
    depth, width = learner.shape[1:]

    def copy(entries_ref, in_ref, out_ref):
        out_ref[...] = in_ref[...]

    return pl.pallas_call(
        copy,
        grid_spec=pltpu.PrefetchScalarGridSpec(
            num_scalar_prefetch=1,
            grid=(entries.shape[0],),
            in_specs=[pl.BlockSpec((1, depth, width), lambda s, e: (e[s], 0, 0))],
            out_specs=pl.BlockSpec((1, depth, width), lambda s, e: (s, 0, 0)),
        ),
        out_shape=jax.ShapeDtypeStruct((entries.shape[0], depth, width), learner.dtype),
    )(entries, learner)


def moe_kernel(
    devices,
    lanes,
    x_ref,
    square_ref,
    share_ref,
    chosen_ref,
    gate_hbm,
    up_hbm,
    down_hbm,
    out_ref,
    held_ref,
    rows,
    squares,
    gate_w,
    up_w,
    down_w,
    parts,
    mid,
    came,
    acts,
    total,
    leaving,
    back,
    local_sem,
    row_send,
    row_recv,
    square_send,
    square_recv,
    part_send,
    part_recv,
    act_send,
    act_recv,
    back_send,
    back_recv,
    held_send,
    held_recv,
):
    i, t = lax.axis_index("expert"), lax.axis_index("tensor")
    per = devices // lanes
    entries, depth, width = gate_w.shape
    row_count = x_ref.shape[1]
    whole = devices * lanes
    me = i * lanes + t

    def remote(src, dst, send, recv, expert, tensor):
        return pltpu.make_async_remote_copy(
            src_ref=src,
            dst_ref=dst,
            send_sem=send,
            recv_sem=recv,
            device_id=(expert, tensor),
            device_id_type=pl.DeviceIdType.MESH,
        )

    def each(first, last, body):
        lax.fori_loop(first, last, lambda k, c: (body(k), c)[1], 0)

    loads = [
        pltpu.make_async_copy(gate_hbm, gate_w, local_sem.at[0]),
        pltpu.make_async_copy(up_hbm, up_w, local_sem.at[1]),
        pltpu.make_async_copy(down_hbm, down_w, local_sem.at[2]),
    ]
    for load in loads:
        load.start()
    own = pltpu.make_async_copy(chosen_ref.at[i], held_ref.at[i], local_sem.at[3])
    own.start()

    barrier = pltpu.get_barrier_semaphore()

    def greet(k):
        other = lax.rem(me + k, whole)
        pl.semaphore_signal(
            barrier,
            inc=1,
            device_id=(other // lanes, lax.rem(other, lanes)),
            device_id_type=pl.DeviceIdType.MESH,
        )

    each(1, whole, greet)
    pl.semaphore_wait(barrier, whole - 1)

    def row_copy(p, k):
        to = lax.rem(t + k, lanes)
        return remote(
            x_ref.at[p], rows.at[i], row_send.at[p * lanes + k], row_recv.at[i], t * per + p, to
        )

    for p in range(per):
        each(1, lanes, lambda k, p=p: row_copy(p, k).start())
        pl.when(t * per + p != i)(lambda p=p: row_copy(p, 0).start())

    def square_copy(k):
        to = lax.rem(t + k, lanes)
        return remote(square_ref, squares.at[t], square_send.at[k], square_recv.at[t], i, to)

    each(1, lanes, lambda k: square_copy(k).start())

    def held_copy(k):
        to = lax.rem(i + k, devices)
        return remote(
            chosen_ref.at[to], held_ref.at[i], held_send.at[k], held_recv.at[i], to, t
        )


    home = i // per

    @pl.when(home == t)
    def _():
        rows[i] = x_ref[lax.rem(i, per)]

    squares[t] = square_ref[...]

    def row_arrival(k):
        origin = lax.rem(i + k, devices)
        remote(
            x_ref.at[0], rows.at[origin], row_send.at[0], row_recv.at[origin], origin, home
        ).wait_recv()

    each(1, devices, row_arrival)
    pl.when(home != t)(lambda: row_arrival(0))
    loads[0].wait()
    loads[1].wait()

    def project(e):
        arrived = rows[...].reshape(devices * row_count, depth)
        for which, weight in enumerate((gate_w, up_w)):
            product = jnp.dot(arrived, weight[e], preferred_element_type=jnp.float32)
            parts[:, which, e] = product.astype(jnp.bfloat16).reshape(devices, row_count, width)

    each(0, entries, project)

    half = devices // 2
    group, side = i // 2, lax.rem(i, 2)
    pair = group * 2 + 1 - side

    def part_copy(k):
        line = lax.rem(group + k, half)
        return remote(
            parts.at[line * 2 + 1 - side],
            mid.at[line],
            part_send.at[k],
            part_recv.at[line],
            pair,
            t,
        )

    each(1, half, lambda k: part_copy(k).start())
    part_copy(0).start()

    def sum_copy(k):
        mine = lax.rem(group + k, half) * 2 + side
        return remote(
            parts.at[mine],
            came.at[group],
            part_send.at[half + k],
            part_recv.at[half + group],
            mine,
            t,
        )

    def part_sum(k):
        line = lax.rem(group + k, half)
        mine = line * 2 + side
        remote(
            parts.at[0], mid.at[line], part_send.at[0], part_recv.at[line], pair, t
        ).wait_recv()

        def add(e):
            both = parts[mine, :, e].astype(jnp.float32) + mid[line, :, e].astype(jnp.float32)
            parts[mine, :, e] = both.astype(jnp.bfloat16)

        each(0, entries, add)

    def part_pass(k):
        part_sum(k)
        sum_copy(k).start()

    each(1, half, part_pass)
    part_sum(0)
    came[group] = parts[i]

    def square_arrival(k):
        origin = lax.rem(t + k, lanes)
        remote(
            square_ref, squares.at[origin], square_send.at[0], square_recv.at[origin], i, origin
        ).wait_recv()

    each(1, lanes, square_arrival)
    features = depth * devices
    row_scale = lax.rsqrt(jnp.sum(squares[...], axis=0) / features + NORM_EPSILON)[:, :1]

    def part_arrival(k):
        line = lax.rem(group + k, half)
        remote(
            parts.at[0],
            came.at[line],
            part_send.at[0],
            part_recv.at[half + line],
            line * 2 + side,
            t,
        ).wait_recv()

    each(1, half, part_arrival)

    def activate(e):
        gate = jnp.sum(came[:, 0, e].astype(jnp.float32), axis=0) * row_scale
        up = jnp.sum(came[:, 1, e].astype(jnp.float32), axis=0) * row_scale
        silu = gate / (1.0 + jnp.exp(-gate))
        acts[i, e] = (silu * up * share_ref[e]).astype(jnp.bfloat16)

    each(0, entries, activate)

    def act_copy(k):
        to = lax.rem(group + k, half) * 2 + side
        return remote(acts.at[i], acts.at[i], act_send.at[k], act_recv.at[i], to, t)

    def pair_copy(k):
        origin = lax.rem(group + k, half) * 2 + side
        return remote(
            acts.at[origin], acts.at[origin], act_send.at[half + k], act_recv.at[origin], pair, t
        )

    each(1, half, lambda k: act_copy(k).start())
    pair_copy(0).start()
    each(1, devices, lambda k: held_copy(k).start())

    def act_arrival(origin):
        remote(
            acts.at[i], acts.at[origin], act_send.at[0], act_recv.at[origin], pair, t
        ).wait_recv()

    def act_pass(k):
        act_arrival(lax.rem(group + k, half) * 2 + side)
        pair_copy(k).start()

    each(1, half, act_pass)
    loads[2].wait()
    each(0, half, lambda k: act_arrival(lax.rem(group + k, half) * 2 + 1 - side))
    total[...] = jnp.zeros_like(total)

    def lower(e):
        total[...] += lax.dot_general(
            acts[:, e].reshape(devices * row_count, width),
            down_w[e],
            (((1,), (1,)), ((), ())),
            preferred_element_type=jnp.float32,
        )

    each(0, entries, lower)
    leaving[...] = total[...].astype(jnp.bfloat16).reshape(devices, row_count, depth)

    place = lax.rem(i, per) * lanes + t

    def back_copy(k):
        to = lax.rem(i + k, devices)
        return remote(leaving.at[to], back.at[place], back_send.at[k], back_recv.at[place], to, home)

    each(1, devices, lambda k: back_copy(k).start())
    pl.when(home != t)(lambda: back_copy(0).start())

    @pl.when(home == t)
    def _():
        back[place] = leaving[i]

    def back_arrival(p, k):
        lane = lax.rem(t + k, lanes)
        slot = p * lanes + lane
        remote(
            leaving.at[0], back.at[slot], back_send.at[0], back_recv.at[slot], t * per + p, lane
        ).wait_recv()

    for p in range(per):
        each(1, lanes, lambda k, p=p: back_arrival(p, k))
        pl.when(t * per + p != i)(lambda p=p: back_arrival(p, 0))
    for p in range(per):
        summed = jnp.zeros((row_count, depth), jnp.float32)
        for lane in range(lanes):
            summed += back[p * lanes + lane].astype(jnp.float32)
        out_ref[p] = summed.astype(jnp.bfloat16)

    for p in range(per):
        each(1, lanes, lambda k, p=p: row_copy(p, k).wait_send())
        pl.when(t * per + p != i)(lambda p=p: row_copy(p, 0).wait_send())
    each(1, lanes, lambda k: square_copy(k).wait_send())
    each(0, half, lambda k: part_copy(k).wait_send())
    each(1, half, lambda k: sum_copy(k).wait_send())
    each(1, half, lambda k: act_copy(k).wait_send())
    each(0, half, lambda k: pair_copy(k).wait_send())
    each(1, devices, lambda k: back_copy(k).wait_send())
    pl.when(home != t)(lambda: back_copy(0).wait_send())

    def held_arrival(k):
        origin = lax.rem(i + k, devices)
        remote(
            chosen_ref.at[0], held_ref.at[origin], held_send.at[0], held_recv.at[origin], origin, t
        ).wait_recv()

    each(1, devices, held_arrival)
    each(1, devices, lambda k: held_copy(k).wait_send())
    own.wait()


def moe(x, square, share, chosen, gate, up, down, devices, lanes):
    entries, depth, width = gate.shape
    per, row_count = x.shape[:2]
    held_each = chosen.shape[1]
    vmem = pl.BlockSpec(memory_space=pltpu.VMEM)
    anywhere = pl.BlockSpec(memory_space=pl.ANY)
    bf16 = jnp.bfloat16
    dma = pltpu.SemaphoreType.DMA
    return pl.pallas_call(
        functools.partial(moe_kernel, devices, lanes),
        out_shape=(
            jax.ShapeDtypeStruct((per, row_count, depth), bf16),
            jax.ShapeDtypeStruct((devices, held_each, depth, width), bf16),
        ),
        in_specs=[vmem, vmem, vmem, anywhere, anywhere, anywhere, anywhere],
        out_specs=(vmem, anywhere),
        scratch_shapes=[
            pltpu.VMEM((devices, row_count, depth), bf16),
            pltpu.VMEM((lanes,) + square.shape, jnp.float32),
            pltpu.VMEM(gate.shape, bf16),
            pltpu.VMEM(up.shape, bf16),
            pltpu.VMEM(down.shape, bf16),
            pltpu.VMEM((devices, 2, entries, row_count, width), bf16),
            pltpu.VMEM((devices // 2, 2, entries, row_count, width), bf16),
            pltpu.VMEM((devices // 2, 2, entries, row_count, width), bf16),
            pltpu.VMEM((devices, entries, row_count, width), bf16),
            pltpu.VMEM((devices * row_count, depth), jnp.float32),
            pltpu.VMEM((devices, row_count, depth), bf16),
            pltpu.VMEM((per * lanes, row_count, depth), bf16),
            dma((4,)),
            dma((per * lanes,)),
            dma((devices,)),
            dma((lanes,)),
            dma((lanes,)),
            dma((devices,)),
            dma((devices,)),
            dma((devices,)),
            dma((devices,)),
            dma((devices,)),
            dma((per * lanes,)),
            dma((devices,)),
            dma((devices,)),
        ],
        compiler_params=pltpu.CompilerParams(
            collective_id=0, has_side_effects=True, vmem_limit_bytes=60 * 1024 * 1024
        ),
        cost_estimate=pl.CostEstimate(
            flops=6 * devices * row_count * entries * depth * width,
            bytes_accessed=10 * entries * depth * width,
            transcendentals=row_count * entries * width,
        ),
    )(x, square, share, chosen, gate, up, down)


def per_device(
    query_latent,
    kv_cache,
    cache_len,
    value_up,
    hidden_in,
    norm_gain,
    expert_ids,
    route_weight,
    placement_plan,
    updated_list,
    learner_gate,
    learner_up,
    learner_down,
):
    expert_total, depth, width = learner_gate.shape
    devices, lanes = lax.axis_size("expert"), lax.axis_size("tensor")
    per = devices // lanes
    row_count = hidden_in.shape[0]
    slot_total = placement_plan.shape[0]
    held_each = slot_total // devices
    entry_range = jnp.arange(expert_total, dtype=jnp.int32)
    learner_entry = jnp.sum(
        entry_range[None, :] * (updated_list[None, :] == placement_plan[:, None]).astype(jnp.int32),
        axis=1,
    )
    chosen_gate = pick_entries(learner_gate, learner_entry).reshape(
        devices, held_each, depth, width
    )
    widened = hidden_in.astype(jnp.float32)
    square = jnp.broadcast_to(jnp.sum(widened * widened, axis=1, keepdims=True), (row_count, 128))
    gained = (widened * norm_gain.astype(jnp.float32)[None, :]).astype(jnp.bfloat16)
    gained = jnp.swapaxes(gained.reshape(row_count, per, depth), 0, 1)
    weights_float = route_weight.astype(jnp.float32)
    gates = ROUTE_SCALE * weights_float / jnp.sum(weights_float, axis=1, keepdims=True)
    named = (expert_ids[None, :, :] == updated_list[:, None, None]).astype(jnp.float32)
    share = jnp.sum(gates[None, :, :] * named, axis=2)
    share = jnp.broadcast_to(share[:, :, None], (expert_total, row_count, width))
    moe_parts, held = moe(
        gained, square, share, chosen_gate, learner_gate, learner_up, learner_down, devices, lanes
    )
    moe_out = jnp.swapaxes(moe_parts, 0, 1).reshape(row_count, per * depth)
    held_gate = jnp.swapaxes(held, 0, 1).reshape(held_each, devices * depth, width)
    latent = attend(query_latent, kv_cache, cache_len)
    head_rows = lax.all_to_all(latent, "tensor", split_axis=1, concat_axis=0, tiled=True)
    projected = jnp.einsum("rhc,hcv->rhv", head_rows, value_up, preferred_element_type=jnp.float32)
    attn_values = projected.astype(jnp.bfloat16).reshape(
        head_rows.shape[0], projected.shape[1] * projected.shape[2]
    )
    return (attn_values, moe_out, held_gate)


def solution(mesh):
    in_specs = (
        P(("expert", "tensor"), None, None),
        P(("expert", "tensor"), None, None),
        P(("expert", "tensor")),
        P("tensor", None, None),
        P("expert", "tensor"),
        P("tensor"),
        P("expert", None),
        P("expert", None),
        P(),
        P(),
        P(None, "expert", "tensor"),
        P(None, "expert", "tensor"),
        P(None, "expert", "tensor"),
    )
    out_specs = (P("expert", "tensor"), P("expert", "tensor"), P("expert", None, "tensor"))
    return jax.shard_map(
        per_device, mesh=mesh, in_specs=in_specs, out_specs=out_specs, check_vma=False
    )
```
